512 devices in a mesh: queue: 64 (over z_lo, x, core), head: 8 (over y, z_hi).
Axes of the slice: x: 4, y: 4, z: 16 (z_hi: 2, z_lo: 8; z = z_hi * 8 + z_lo), core: 2. Of those that a mesh axis runs over, the one named last changes fastest.
Arguments:
- residual: bfloat16 [32768, 5120], P('queue', 'head'), may hold values from -3 to 3
- queries: bfloat16 [32768, 5120], P('queue', 'head'), may hold values from -1000 to 1000
- keys: bfloat16 [32768, 5120], P('queue', 'head'), may hold values from -4 to 4
- values: bfloat16 [32768, 5120], P('queue', 'head'), may hold values from -6 to 6
- out_weight: bfloat16 [5120, 5120], P('queue', 'head'), may hold values from -0.078125 to 0.078125
- gate_table: float32 [64, 5120], P(None, 'head'), may hold values from 0.5 to 2
- levels: int32 [64], P('queue'), may hold values from 0 to 63, each once
Outputs:
- mixed: bfloat16 [32768, 5120], P('queue', 'head')
The draws below stay inside these ranges and needn't reach their ends.
All inputs are finite; a program needn't handle non-finite values.
Results may differ from the reference program's by a relative error of at most 0.0034.
Values may be sent and summed in bfloat16 or wider, within the bound.
A program may use at most 64 MiB of HBM per device.

```python
import math
import jax
import jax.numpy as jnp
from jax import lax

D = 5120
HD = 128
GROUP_TOK = 512
HEADS = 40
GROUPS = 64
TOKENS = 32768


def drawn_keys(key):
    base = jax.random.normal(jax.random.fold_in(key, 11), (TOKENS, HEADS * HD), jnp.float32)
    base = jnp.clip(base, -4.0, 4.0)
    return base


def draw_keys(key, part):
    base = drawn_keys(key)
    return base.astype(jnp.bfloat16)


def draw_queries(key, part):
    key = jax.random.fold_in(key, 5)
    return (2.0 * jnp.clip(jax.random.normal(key, (TOKENS, HEADS * HD), jnp.float32), -4.0, 4.0)).astype(jnp.bfloat16)


def block_scale(own_key, extent, pieces, least, high):
    factor_of, own = 1.0, jax.random.fold_in(own_key, 6)
    for dim, shards_of in pieces:
        steps = jnp.exp(jax.random.uniform(jax.random.fold_in(own, dim), (shards_of,), jnp.float32, least / len(pieces), high / len(pieces)))
        factor_of = factor_of * jnp.repeat(steps, extent[dim] // shards_of).reshape([-1 if axis == dim else 1 for axis in range(len(extent))])
    return factor_of


def centred(key, shape, scale, most, pieces=(), held_as=jnp.bfloat16):
    values = jax.random.normal(key, shape, jnp.float32) * scale
    if len(pieces) > 0:
        values = block_scale(key, shape, pieces, -0.22, 0.18) * values
    return jnp.clip(values, min=-most, max=most).astype(held_as)


def setup_inputs(seed: int = 0) -> dict:
    key_list = jax.random.split(jax.random.key(seed), 8)
    residual = centred(key_list[0], (TOKENS, D), 0.5, 3.0, ((0, 64), (1, 8)))
    queries = draw_queries(jax.random.fold_in(key_list[7], 71), 0)
    keys = draw_keys(jax.random.fold_in(key_list[7], 71), 0)
    values = centred(key_list[3], (TOKENS, HEADS * HD), 1.0, 6.0, ((0, 64), (1, 8)))
    out_weight = centred(key_list[4], (HEADS * HD, D), (HEADS * HD) ** -0.5, 0.078125, ((0, 64), (1, 8)))
    gate_table = jnp.clip(0.5 + 1.5 * jax.random.uniform(key_list[5], (GROUPS, D), jnp.float32) ** block_scale(key_list[5], (GROUPS, D), ((1, 8),), -0.2, 0.2), 0.5, 2.0)
    levels = jax.random.permutation(key_list[6], GROUPS).astype(jnp.int32)
    return dict(residual=residual, queries=queries, keys=keys, values=values, out_weight=out_weight, gate_table=gate_table, levels=levels)


def reference(residual, queries, keys, values, out_weight, gate_table, levels):
    head_count = HEADS
    shape_four = (GROUPS, GROUP_TOK, head_count, HD)
    query_four = queries.reshape(shape_four)
    key_four = keys.reshape(shape_four)
    value_four = values.reshape(shape_four)
    zero_group = jnp.zeros((1, GROUP_TOK, head_count, HD), keys.dtype)
    prior_key_four = jnp.concatenate([zero_group, key_four[:-1]], axis=0)
    prior_value_four = jnp.concatenate([zero_group, value_four[:-1]], axis=0)
    group_ids = jnp.arange(GROUPS, dtype=jnp.int32)
    score_scale = 1.0 / math.sqrt(HD)

    def one_group(items):
        query_group, key_group, value_group, prior_key, prior_value, group_id = items
        all_keys = jnp.concatenate([prior_key, key_group], axis=0).astype(jnp.float32)
        all_values = jnp.concatenate([prior_value, value_group], axis=0).astype(jnp.float32)
        scores = jnp.einsum('qhd,khd->hqk', query_group.astype(jnp.float32), all_keys) * score_scale
        column = jnp.arange(2 * GROUP_TOK, dtype=jnp.int32)
        blocked = (group_id == 0) & (column < GROUP_TOK)
        scores = jnp.where(blocked[None, None, :], -jnp.inf, scores)
        row_max = lax.optimization_barrier(jnp.max(scores, axis=2, keepdims=True))
        weights = jnp.exp(scores - row_max)
        totals = lax.optimization_barrier(jnp.sum(weights, axis=2, keepdims=True))
        probs = lax.optimization_barrier(weights.astype(jnp.bfloat16)).astype(jnp.float32)
        summed = jnp.einsum('hqk,khd->qhd', probs, all_values)
        return (summed / jnp.transpose(totals, (1, 0, 2))).astype(jnp.bfloat16)
    attended = lax.map(one_group, (query_four, key_four, value_four, prior_key_four, prior_value_four, group_ids))
    attended = attended.reshape(TOKENS, head_count * HD)
    projected = jnp.dot(attended, out_weight, preferred_element_type=jnp.float32)
    gate_rows = gate_table[levels]
    result = residual.astype(jnp.float32).reshape(GROUPS, GROUP_TOK, D) + gate_rows[:, None, :] * projected.reshape(GROUPS, GROUP_TOK, D)
    return result.astype(jnp.bfloat16).reshape(TOKENS, D)
```

```python
import functools
import math

import jax
import jax.numpy as jnp
from jax import lax
from jax.experimental import pallas as pl
from jax.experimental.pallas import tpu as pltpu
from jax.sharding import PartitionSpec as P

HD = 128
XS, YS, CORES, ZH = 4, 4, 2, 2
MESH = pl.DeviceIdType.MESH
ROWS = 256


def kernel(
    zl_count,
    res_hbm, q_hbm, k_hbm, v_hbm, w_hbm, gate_ref, level_ref,
    out_hbm,
    q_ref, k_ref, v_ref, res_ref, out_ref, pk_ref, pv_ref, w_ref, a_ref, acc_ref,
    load_sem, store_sem,
    kv_send, kv_recv, wz_up, wz_down, wz_recv, wx_send, wx_recv, ws_send, ws_recv,
    az_send, az_recv, ay_send, ay_own, ay_far,
):
    tokens, width = q_ref.shape
    heads = width // HD
    parts = tokens // ROWS
    pieces = heads * parts
    depth = w_hbm.shape[0]
    queue_count = zl_count * XS * CORES

    queue = lax.axis_index("queue")
    head = lax.axis_index("head")
    core = lax.rem(queue, CORES)
    x = lax.rem(queue // CORES, XS)
    zl = queue // (CORES * XS)
    y = head // ZH
    zh = lax.rem(head, ZH)

    sibling = (queue + 1 - 2 * core, head)
    partner = (queue, head + 1 - 2 * zh)
    far = head + 1 - 2 * zh

    def x_peer(k):
        return (queue + CORES * (lax.rem(x + k, XS) - x), head)

    def y_peer(k):
        return (queue, head + ZH * (lax.rem(y + k, YS) - y))

    up, down = (queue + CORES * XS, head), (queue - CORES * XS, head)
    after, before = (queue + 1, head), (queue - 1, head)
    has_up, has_down = zl < zl_count - 1, zl > 0
    has_after, has_before = queue < queue_count - 1, queue > 0

    def remote(src, dst, send, recv, device):
        return pltpu.make_async_remote_copy(
            src_ref=src, dst_ref=dst, send_sem=send, recv_sem=recv, device_id=device, device_id_type=MESH
        )

    def landed(ref, sem):
        pltpu.make_async_copy(ref, ref, sem).wait()

    loads = [
        pltpu.make_async_copy(src, dst, load_sem.at[i])
        for i, (src, dst) in enumerate(((q_hbm, q_ref), (k_hbm, k_ref), (v_hbm, v_ref), (res_hbm, res_ref)))
    ]
    for load in loads:
        load.start()
    block = pl.multiple_of(queue * depth, 16)
    own_w = pltpu.make_async_copy(w_hbm, w_ref.at[pl.ds(block, depth)], load_sem.at[4])
    own_w.start()

    barrier = pltpu.get_barrier_semaphore()
    greet = [sibling, partner] + [x_peer(k) for k in (1, 2, 3)] + [y_peer(k) for k in (1, 2, 3)]
    for device in greet:
        pl.semaphore_signal(barrier, inc=1, device_id=device, device_id_type=MESH)
    for there, device in ((has_up, up), (has_down, down), (has_after, after), (has_before, before)):
        @pl.when(there)
        def _():
            pl.semaphore_signal(barrier, inc=1, device_id=device, device_id_type=MESH)
    edges = sum(there.astype(jnp.int32) for there in (has_up, has_down, has_after, has_before))
    pl.semaphore_wait(barrier, len(greet) + edges)

    @pl.when(has_after)
    def _():
        for h in range(heads):
            columns = pl.ds(h * HD, HD)
            remote(k_hbm.at[:, columns], pk_ref.at[h], kv_send, kv_recv.at[0, h], after).start()
            remote(v_hbm.at[:, columns], pv_ref.at[h], kv_send, kv_recv.at[1, h], after).start()

    def w_rows(zl_from, x_from, core_from):
        index = (zl_from * XS + x_from) * CORES + core_from
        return w_ref.at[pl.ds(pl.multiple_of(index * depth, 16), depth)]

    def w_up(zl_from, src):
        remote(src, w_rows(zl_from, x, core), wz_up.at[zl_from], wz_recv.at[zl_from], up).start()

    def w_down(zl_from, src):
        remote(src, w_rows(zl_from, x, core), wz_down.at[zl_from], wz_recv.at[zl_from], down).start()

    def w_across(zl_from, src):
        dst = w_rows(zl_from, x, core)
        for k in (1, 3, 2):
            remote(src, dst, wx_send, wx_recv.at[k - 1], x_peer(k)).start()
        remote(src, dst, ws_send, ws_recv, sibling).start()

    @pl.when(has_up)
    def _():
        w_up(zl, w_hbm)

    @pl.when(has_down)
    def _():
        w_down(zl, w_hbm)

    def w_step(t):
        low, high = zl - t, zl + t

        @pl.when(low >= 0)
        def _():
            rows = w_rows(low, x, core)
            landed(rows, wz_recv.at[low])

            @pl.when(has_up)
            def _():
                w_up(low, rows)

            w_across(low, rows)

        @pl.when(high < zl_count)
        def _():
            rows = w_rows(high, x, core)
            landed(rows, wz_recv.at[high])

            @pl.when(has_down)
            def _():
                w_down(high, rows)

            w_across(high, rows)

    @pl.when(jnp.logical_not(has_before))
    def _():
        pk_ref[...] = jnp.zeros_like(pk_ref)
        pv_ref[...] = jnp.zeros_like(pv_ref)

    levels = lax.broadcasted_iota(jnp.int32, gate_ref.shape, 0)
    gate_row = jnp.sum(jnp.where(levels == level_ref[0], gate_ref[...], 0.0), axis=0, keepdims=True)
    blocked = jnp.where(has_before, 0.0, -1e30).astype(jnp.float32)

    for load in loads:
        load.wait()
    own_w.wait()

    def piece(source, p):
        h, part = p // parts, p % parts
        return a_ref.at[source, h, pl.ds(part * ROWS, ROWS)]

    scale = math.log2(math.e) / math.sqrt(HD)
    contract_last = (((1,), (1,)), ((), ()))
    for h in range(heads):
        columns = pl.ds(h * HD, HD)

        @pl.when(has_before)
        def _():
            landed(pk_ref.at[h], kv_recv.at[0, h])
            landed(pv_ref.at[h], kv_recv.at[1, h])

        for part in range(parts):
            rows = pl.ds(part * ROWS, ROWS)
            queries = q_ref[rows, columns]
            own = lax.dot_general(queries, k_ref[:, columns], contract_last, preferred_element_type=jnp.float32) * scale
            prior = lax.dot_general(queries, pk_ref[h], contract_last, preferred_element_type=jnp.float32) * scale + blocked
            row_max = jnp.maximum(jnp.max(own, axis=1, keepdims=True), jnp.max(prior, axis=1, keepdims=True))
            own = jnp.exp2(own - row_max)
            prior = jnp.exp2(prior - row_max)
            totals = jnp.sum(own, axis=1, keepdims=True) + jnp.sum(prior, axis=1, keepdims=True)
            summed = jnp.dot(own.astype(jnp.bfloat16), v_ref[:, columns], preferred_element_type=jnp.float32)
            summed += jnp.dot(prior.astype(jnp.bfloat16), pv_ref[h], preferred_element_type=jnp.float32)
            a_ref[head, h, rows] = (summed / totals).astype(jnp.bfloat16)
            p = h * parts + part
            remote(piece(head, p), piece(head, p), az_send, az_recv.at[p], partner).start()
            for k in (1, 3, 2):
                remote(piece(head, p), piece(head, p), ay_send, ay_own.at[k - 1], y_peer(k)).start()
        if h == 0:
            w_across(zl, w_hbm)
        else:
            w_step(h)
    for t in range(heads, zl_count):
        w_step(t)

    def w_pass(k):
        landed(w_ref.at[pl.ds(0, zl_count * depth)], wx_recv.at[k - 1])
        for zl_from in range(zl_count):
            rows = w_rows(zl_from, lax.rem(x + XS - k, XS), core)
            remote(rows, rows, ws_send, ws_recv, sibling).start()

    def project(source, first_head, last_head, part, first=False):
        rows = pl.ds(part * ROWS, ROWS)
        deep = (last_head - first_head) * HD
        left = jnp.concatenate([a_ref[source, h, rows] for h in range(first_head, last_head)], axis=1)
        start = pl.multiple_of(source * width + first_head * HD, HD)
        term = jnp.dot(left, w_ref[pl.ds(start, deep)], preferred_element_type=jnp.float32)
        if first:
            acc_ref[rows] = term
        else:
            acc_ref[rows] += term

    def far_landed(k, p):
        landed(piece(far, p), ay_far.at[k - 1, p])

    def far_of(k):
        return ZH * lax.rem(y + YS - k, YS) + 1 - zh

    early = (heads - 1) * parts
    for p in range(pieces):
        landed(piece(far, p), az_recv.at[p])
        for k in (1, 3, 2):
            remote(piece(far, p), piece(far, p), ay_send, ay_far.at[k - 1, p], y_peer(k)).start()
        if p in (pieces - 5, pieces - 4, pieces - 3):
            w_pass((1, 3, 2)[p - (pieces - 5)])
        if p == pieces - 2:
            landed(w_ref.at[pl.ds(0, queue_count * depth // 2)], ws_recv)
            for part in range(parts):
                project(head, 0, heads, part, first=True)
            for k in (1, 2, 3):
                landed(a_ref.at[0], ay_own.at[k - 1])
                for part in range(parts):
                    project(ZH * lax.rem(y + YS - k, YS) + zh, 0, heads, part)
            for part in range(parts):
                project(far, 0, heads - 1, part)
            for k in (1, 3, 2):
                for e in range(early):
                    far_landed(k, e)
                for part in range(parts):
                    project(far_of(k), 0, heads - 1, part)
    stores = []
    for part in range(parts):
        project(far, heads - 1, heads, part)
        for k in (1, 3, 2):
            far_landed(k, early + part)
            project(far_of(k), heads - 1, heads, part)
        rows = pl.ds(part * ROWS, ROWS)
        out_ref[rows] = (res_ref[rows].astype(jnp.float32) + gate_row * acc_ref[rows]).astype(jnp.bfloat16)
        store = pltpu.make_async_copy(out_ref.at[rows], out_hbm.at[rows], store_sem.at[part])
        store.start()
        stores.append(store)

    @pl.when(has_after)
    def _():
        landed(w_ref.at[pl.ds(0, 2 * tokens)], kv_send)

    for t in range(zl_count):
        @pl.when(jnp.logical_and(has_up, zl >= t))
        def _():
            landed(w_rows(t, x, core), wz_up.at[t])

        @pl.when(jnp.logical_and(has_down, zl <= t))
        def _():
            landed(w_rows(t, x, core), wz_down.at[t])

    landed(w_ref.at[pl.ds(0, 3 * zl_count * depth)], wx_send)
    landed(w_ref.at[pl.ds(0, XS * zl_count * depth)], ws_send)
    landed(a_ref.at[0], az_send)
    landed(a_ref.at[pl.ds(0, 6)], ay_send)
    for store in stores:
        store.wait()


def shards(residual, queries, keys, values, out_weight, gate_table, levels):
    tokens, width = queries.shape
    heads = width // HD
    pieces = heads * (tokens // ROWS)
    sources = lax.axis_size("head")
    queue_count = lax.axis_size("queue")
    zl_count = queue_count // (XS * CORES)
    whole = out_weight.shape[0] * queue_count
    bf16 = jnp.bfloat16
    dma = pltpu.SemaphoreType.DMA
    anywhere = pl.BlockSpec(memory_space=pl.ANY)
    return pl.pallas_call(
        functools.partial(kernel, zl_count),
        out_shape=jax.ShapeDtypeStruct(residual.shape, bf16),
        in_specs=[anywhere] * 5 + [pl.BlockSpec(memory_space=pltpu.VMEM), pl.BlockSpec(memory_space=pltpu.SMEM)],
        out_specs=anywhere,
        scratch_shapes=[
            pltpu.VMEM((tokens, width), bf16),
            pltpu.VMEM((tokens, width), bf16),
            pltpu.VMEM((tokens, width), bf16),
            pltpu.VMEM((tokens, width), bf16),
            pltpu.VMEM((tokens, width), bf16),
            pltpu.VMEM((heads, tokens, HD), bf16),
            pltpu.VMEM((heads, tokens, HD), bf16),
            pltpu.VMEM((whole, width), bf16),
            pltpu.VMEM((sources, heads, tokens, HD), bf16),
            pltpu.VMEM((tokens, width), jnp.float32),
            dma((5,)),
            dma((tokens // ROWS,)),
            dma,
            dma((2, heads)),
            dma((zl_count,)),
            dma((zl_count,)),
            dma((zl_count,)),
            dma,
            dma((3,)),
            dma,
            dma,
            dma,
            dma((pieces,)),
            dma,
            dma((3,)),
            dma((3, pieces)),
        ],
        compiler_params=pltpu.CompilerParams(
            collective_id=0, has_side_effects=True, vmem_limit_bytes=56 * 2**20
        ),
    )(residual, queries, keys, values, out_weight, gate_table, levels)


def solution(mesh):
    placed = (
        P("queue", "head"),
        P("queue", "head"),
        P("queue", "head"),
        P("queue", "head"),
        P("queue", "head"),
        P(None, "head"),
        P("queue"),
    )
    return jax.shard_map(
        shards, mesh=mesh, in_specs=placed, out_specs=P("queue", "head"), check_vma=False
    )
```

```python
import functools
import math

import jax
import jax.numpy as jnp
from jax import lax
from jax.experimental import pallas as pl
from jax.experimental.pallas import tpu as pltpu
from jax.sharding import PartitionSpec as P

HD = 128
XS, YS, CORES, ZH = 4, 4, 2, 2
MESH = pl.DeviceIdType.MESH
ROWS = 256
HOPS = 8
STEPS = (
    "w0 w1 x30 a0", "r0 z00 r1 a1", "r2 z10 a2 w2", "r3 x31 z01 Y0", "a3 r4 z11 Y1", "x20 z20 z30 Y2", "a4 w3 x32 a5", "z02 z12 Y3 x21", "a6 z21 z31 a7", "w4 x33 Y4 Y5", "x10 a8 z03 z13", "z22 z32 Y6 x22", "x11 a9 x34 Y7", "w5 x12 z04 z14", "Y8 x23 x13 z23", "z33 Y9 x24 x14", "w6 x35 x15 z05", "z15 z24 z34 x36", "x16 w7 z40 z50", "x25 z06 z16 z25", "z35 x26 x17 z41", "z51 x37 z07 z17", "z26 z36 z42 z52", "x27 f0 f1 z60", "z70 z27 z37 o0", "F0 z43 z53 o1", "F1 z61 z71 o2", "f2 f3 z80 z90", "o3 z44 z54 z62", "z72 F2 z81 z91", "F3 g010 z45 z55", "g011 g013 z63 z73", "g012 z82 z92 z46", "z56 z64 z74 z83", "z93 z47 z57 z65", "z75 z84 z94 f4", "f5 z66 z76 z85", "F4 z95 z67 F5", "z77 z86 z96 f6", "f7 z87 z97 F6", "f8 F7 f9 g230", "g231 g233 F8 g232", "F9",
)


def kernel(
    zl_count,
    res_hbm, q_hbm, k_hbm, v_hbm, w_hbm, gate_ref, level_ref,
    out_hbm,
    q_ref, k_ref, v_ref, res_ref, out_ref, pk_ref, pv_ref, relay_ref, w_ref, a_ref, hop_ref, acc_ref,
    load_sem, store_sem,
    kv_send, kv_recv, relay_send, relay_recv, wz_up, wz_down, wz_recv, wx_send, wx_recv, ws_send, ws_recv,
    hop_send, hop_recv, ay_send, ay_own, ay_far,
):
    tokens, width = q_ref.shape
    heads = width // HD
    parts = tokens // ROWS
    pieces = heads * parts
    depth = w_hbm.shape[0]
    queue_count = zl_count * XS * CORES

    queue = lax.axis_index("queue")
    head = lax.axis_index("head")
    core = lax.rem(queue, CORES)
    x = lax.rem(queue // CORES, XS)
    zl = queue // (CORES * XS)
    y = head // ZH
    zh = lax.rem(head, ZH)

    sibling = (queue + 1 - 2 * core, head)
    far = head + 1 - 2 * zh

    def x_peer(k):
        return (queue + CORES * (lax.rem(x + k, XS) - x), head)

    def y_peer(k):
        return (queue, head + ZH * (lax.rem(y + k, YS) - y))

    def ring_peer(way):
        z = lax.rem(zh * zl_count + zl + way + ZH * zl_count, ZH * zl_count)
        there = z // zl_count
        return (queue + CORES * XS * (lax.rem(z, zl_count) - zl), head + there - zh), y * ZH + 1 - there

    up, down = (queue + CORES * XS, head), (queue - CORES * XS, head)
    after, before = (queue + 1, head), (queue - 1, head)
    has_up, has_down = zl < zl_count - 1, zl > 0
    has_after, has_before = queue < queue_count - 1, queue > 0
    crosses = (core == 1) & (x == XS - 1) & has_up
    by_x = (core == 1) & (x == 0) & has_up
    by_z = (core == 1) & (x == XS - 1) & has_down
    crossed = (core == 0) & (x == 0) & has_down
    over = CORES * XS - 1
    forward, back = (queue + over, head), (queue - over, head)

    def remote(src, dst, send, recv, device):
        return pltpu.make_async_remote_copy(
            src_ref=src, dst_ref=dst, send_sem=send, recv_sem=recv, device_id=device, device_id_type=MESH
        )

    def landed(ref, sem):
        pltpu.make_async_copy(ref, ref, sem).wait()

    loads = [
        pltpu.make_async_copy(src, dst, load_sem.at[i])
        for i, (src, dst) in enumerate(((q_hbm, q_ref), (k_hbm, k_ref), (v_hbm, v_ref), (res_hbm, res_ref)))
    ]
    for load in loads:
        load.start()
    block = pl.multiple_of(queue * depth, 16)
    own_w = pltpu.make_async_copy(w_hbm, w_ref.at[pl.ds(block, depth)], load_sem.at[4])
    own_w.start()

    barrier = pltpu.get_barrier_semaphore()
    greet = [sibling, ring_peer(1)[0], ring_peer(-1)[0]] + [x_peer(k) for k in (1, 3)] + [y_peer(k) for k in (1, 3)]
    for device in greet:
        pl.semaphore_signal(barrier, inc=1, device_id=device, device_id_type=MESH)
    edges = (
        (has_after, after), (has_before, before),
        (by_x | crossed, forward), (by_z | crossed, back),
    )
    for there, device in edges:
        @pl.when(there)
        def _():
            pl.semaphore_signal(barrier, inc=1, device_id=device, device_id_type=MESH)
    pl.semaphore_wait(barrier, len(greet) + sum(there.astype(jnp.int32) for there, _ in edges))

    @pl.when(has_after & jnp.logical_not(crosses))
    def _():
        for h in range(heads):
            columns = pl.ds(h * HD, HD)
            remote(k_hbm.at[:, columns], pk_ref.at[h], kv_send, kv_recv.at[0, h], after).start()
            remote(v_hbm.at[:, columns], pv_ref.at[h], kv_send, kv_recv.at[1, h], after).start()

    @pl.when(crosses)
    def _():
        for h in range(heads):
            columns = pl.ds(h * HD, HD)
            remote(k_hbm.at[:, columns], relay_ref.at[h], kv_send, relay_recv.at[h], x_peer(1)).start()
            remote(v_hbm.at[:, columns], relay_ref.at[h], kv_send, relay_recv.at[h], up).start()

    def pass_on(h):
        @pl.when(by_x)
        def _():
            landed(relay_ref.at[h], relay_recv.at[h])
            remote(relay_ref.at[h], pk_ref.at[h], relay_send, kv_recv.at[0, h], forward).start()

        @pl.when(by_z)
        def _():
            landed(relay_ref.at[h], relay_recv.at[h])
            remote(relay_ref.at[h], pv_ref.at[h], relay_send, kv_recv.at[1, h], back).start()

    def w_rows(zl_from, x_from, core_from):
        index = (zl_from * XS + x_from) * CORES + core_from
        return w_ref.at[pl.ds(pl.multiple_of(index * depth, 16), depth)]

    def w_up(zl_from, src):
        @pl.when(has_up)
        def _():
            remote(src, w_rows(zl_from, x, core), wz_up.at[zl_from], wz_recv.at[zl_from], up).start()

    def w_down(zl_from, src):
        @pl.when(has_down)
        def _():
            remote(src, w_rows(zl_from, x, core), wz_down.at[zl_from], wz_recv.at[zl_from], down).start()

    def w_across(zl_from, src):
        dst = w_rows(zl_from, x, core)
        for k in (1, 3):
            remote(src, dst, wx_send, wx_recv.at[k - 1, zl_from], x_peer(k)).start()
        remote(src, dst, ws_send, ws_recv, sibling).start()

    w_up(zl, w_hbm)
    w_down(zl, w_hbm)

    def w_both(t, work):
        @pl.when(zl >= t)
        def _():
            work(zl - t, w_up)

        if t > 0:
            @pl.when(zl + t < zl_count)
            def _():
                work(zl + t, w_down)

    def w_hop(t):
        def work(zl_from, onward):
            rows = w_rows(zl_from, x, core)
            landed(rows, wz_recv.at[zl_from])
            onward(zl_from, rows)
            w_across(zl_from, rows)

        if t == 0:
            w_across(zl, w_hbm)
        else:
            w_both(t, work)

    def w_pass(k, t):
        def work(zl_from, _):
            rows = w_rows(zl_from, lax.rem(x + XS - k, XS), core)
            landed(rows, wx_recv.at[k - 1, zl_from])
            if k == 3:
                remote(rows, rows, wx_send, wx_recv.at[1, zl_from], x_peer(3)).start()
            remote(rows, rows, ws_send, ws_recv, sibling).start()

        w_both(t, work)

    @pl.when(jnp.logical_not(has_before))
    def _():
        pk_ref[...] = jnp.zeros_like(pk_ref)
        pv_ref[...] = jnp.zeros_like(pv_ref)

    levels = lax.broadcasted_iota(jnp.int32, gate_ref.shape, 0)
    gate_row = jnp.sum(jnp.where(levels == level_ref[0], gate_ref[...], 0.0), axis=0, keepdims=True)
    blocked = jnp.where(has_before, 0.0, -1e30).astype(jnp.float32)

    for load in loads:
        load.wait()
    own_w.wait()

    def piece(source, p):
        h, part = p // parts, p % parts
        return a_ref.at[source, h, pl.ds(part * ROWS, ROWS)]

    def z_hop(p, hop):
        device, last = ring_peer(1 - 2 * (p % 2))
        src = piece(head, p)
        if hop > 0:
            src = hop_ref.at[p, hop - 1]
            landed(src, hop_recv.at[p, hop - 1])
        dst = hop_ref.at[p, hop] if hop < HOPS - 1 else piece(last, p)
        remote(src, dst, hop_send, hop_recv.at[p, hop], device).start()

    def y_send(source, p, arrived):
        for k in (1, 3):
            remote(piece(source, p), piece(source, p), ay_send, arrived.at[k - 1, p], y_peer(k)).start()

    scale = math.log2(math.e) / math.sqrt(HD)
    contract_last = (((1,), (1,)), ((), ()))

    def attend(p):
        h, part = p // parts, p % parts
        columns = pl.ds(h * HD, HD)
        rows = pl.ds(part * ROWS, ROWS)
        if part == 0:
            @pl.when(has_before)
            def _():
                landed(pk_ref.at[h], kv_recv.at[0, h])
                landed(pv_ref.at[h], kv_recv.at[1, h])

        queries = q_ref[rows, columns]
        own = lax.dot_general(queries, k_ref[:, columns], contract_last, preferred_element_type=jnp.float32) * scale
        prior = lax.dot_general(queries, pk_ref[h], contract_last, preferred_element_type=jnp.float32) * scale + blocked
        row_max = jnp.maximum(jnp.max(own, axis=1, keepdims=True), jnp.max(prior, axis=1, keepdims=True))
        own = jnp.exp2(own - row_max)
        prior = jnp.exp2(prior - row_max)
        totals = jnp.sum(own, axis=1, keepdims=True) + jnp.sum(prior, axis=1, keepdims=True)
        summed = jnp.dot(own.astype(jnp.bfloat16), v_ref[:, columns], preferred_element_type=jnp.float32)
        summed += jnp.dot(prior.astype(jnp.bfloat16), pv_ref[h], preferred_element_type=jnp.float32)
        a_ref[head, h, rows] = (summed / totals).astype(jnp.bfloat16)
        y_send(head, p, ay_own)

    def project(source, first_head, last_head, part, first=False):
        rows = pl.ds(part * ROWS, ROWS)
        deep = (last_head - first_head) * HD
        left = jnp.concatenate([a_ref[source, h, rows] for h in range(first_head, last_head)], axis=1)
        start = pl.multiple_of(source * width + first_head * HD, HD)
        term = jnp.dot(left, w_ref[pl.ds(start, deep)], preferred_element_type=jnp.float32)
        if first:
            acc_ref[rows] = term
        else:
            acc_ref[rows] += term

    def source_of(k, side):
        return ZH * lax.rem(y + YS - k, YS) + side

    seen = set()

    def y_landed(k, side, p):
        if k > 0 and (k, side is zh, p) not in seen:
            seen.add((k, side is zh, p))
            landed(piece(source_of(k, side), p), (ay_own if side is zh else ay_far).at[k - 1, p])

    def y_pass(side, p):
        k = 1 if p % 2 == 0 else 3
        y_landed(k, side, p)
        ref = piece(source_of(k, side), p)
        arrived = ay_own if side is zh else ay_far
        remote(ref, ref, ay_send, arrived.at[1, p], y_peer(k)).start()

    def project_source(k, side, first_head, last_head, part, first=False):
        for h in range(first_head, last_head):
            y_landed(k, side, h * parts + part)
        project(source_of(k, side), first_head, last_head, part, first)

    other = 1 - zh
    weights_here = False
    for step in " ".join(STEPS).split():
        kind, numbers = step[0], [int(c) for c in step[1:]]
        if kind == "a":
            attend(*numbers)
        elif kind == "r":
            pass_on(*numbers)
        elif kind == "z":
            z_hop(*numbers)
        elif kind == "f":
            landed(piece(far, numbers[0]), hop_recv.at[numbers[0], HOPS - 1])
            y_send(far, numbers[0], ay_far)
        elif kind == "Y":
            y_pass(zh, *numbers)
        elif kind == "F":
            y_pass(other, *numbers)
        elif kind == "w":
            w_hop(*numbers)
        elif kind == "x":
            w_pass(*numbers)
        else:
            if not weights_here:
                landed(w_ref.at[pl.ds(0, queue_count * depth // 2)], ws_recv)
                weights_here = True
            for part in range(parts):
                if kind == "o":
                    project_source(numbers[0], zh, 0, heads, part, first=numbers[0] == 0)
                else:
                    project_source(numbers[2], other, numbers[0], numbers[1] + 1, part)
    stores = []
    for part in range(parts):
        for k in (0, 1, 3, 2):
            project_source(k, other, heads - 1, heads, part)
        rows = pl.ds(part * ROWS, ROWS)
        out_ref[rows] = (res_ref[rows].astype(jnp.float32) + gate_row * acc_ref[rows]).astype(jnp.bfloat16)
        store = pltpu.make_async_copy(out_ref.at[rows], out_hbm.at[rows], store_sem.at[part])
        store.start()
        stores.append(store)

    @pl.when(by_x | by_z)
    def _():
        landed(relay_ref, relay_send)

    @pl.when(has_after)
    def _():
        landed(w_ref.at[pl.ds(0, 2 * tokens)], kv_send)

    for t in range(zl_count):
        @pl.when(has_up & (zl >= t))
        def _():
            landed(w_rows(t, x, core), wz_up.at[t])

        @pl.when(has_down & (zl <= t))
        def _():
            landed(w_rows(t, x, core), wz_down.at[t])

    landed(w_ref.at[pl.ds(0, 3 * zl_count * depth)], wx_send)
    landed(w_ref.at[pl.ds(0, XS * zl_count * depth)], ws_send)
    landed(a_ref, hop_send)
    landed(a_ref.at[pl.ds(0, 6)], ay_send)
    for store in stores:
        store.wait()


def shards(residual, queries, keys, values, out_weight, gate_table, levels):
    tokens, width = queries.shape
    heads = width // HD
    pieces = heads * (tokens // ROWS)
    sources = lax.axis_size("head")
    queue_count = lax.axis_size("queue")
    zl_count = queue_count // (XS * CORES)
    whole = out_weight.shape[0] * queue_count
    bf16 = jnp.bfloat16
    dma = pltpu.SemaphoreType.DMA
    anywhere = pl.BlockSpec(memory_space=pl.ANY)
    return pl.pallas_call(
        functools.partial(kernel, zl_count),
        out_shape=jax.ShapeDtypeStruct(residual.shape, bf16),
        in_specs=[anywhere] * 5 + [pl.BlockSpec(memory_space=pltpu.VMEM), pl.BlockSpec(memory_space=pltpu.SMEM)],
        out_specs=anywhere,
        scratch_shapes=[
            pltpu.VMEM((tokens, width), bf16),
            pltpu.VMEM((tokens, width), bf16),
            pltpu.VMEM((tokens, width), bf16),
            pltpu.VMEM((tokens, width), bf16),
            pltpu.VMEM((tokens, width), bf16),
            pltpu.VMEM((heads, tokens, HD), bf16),
            pltpu.VMEM((heads, tokens, HD), bf16),
            pltpu.VMEM((heads, tokens, HD), bf16),
            pltpu.VMEM((whole, width), bf16),
            pltpu.VMEM((sources, heads, tokens, HD), bf16),
            pltpu.VMEM((pieces, HOPS - 1, ROWS, HD), bf16),
            pltpu.VMEM((tokens, width), jnp.float32),
            dma((5,)),
            dma((tokens // ROWS,)),
            dma,
            dma((2, heads)),
            dma,
            dma((heads,)),
            dma((zl_count,)),
            dma((zl_count,)),
            dma((zl_count,)),
            dma,
            dma((3, zl_count)),
            dma,
            dma,
            dma,
            dma((pieces, HOPS)),
            dma,
            dma((3, pieces)),
            dma((3, pieces)),
        ],
        compiler_params=pltpu.CompilerParams(
            collective_id=0, has_side_effects=True, vmem_limit_bytes=56 * 2**20
        ),
    )(residual, queries, keys, values, out_weight, gate_table, levels)


def solution(mesh):
    placed = (
        P("queue", "head"),
        P("queue", "head"),
        P("queue", "head"),
        P("queue", "head"),
        P("queue", "head"),
        P(None, "head"),
        P("queue"),
    )
    return jax.shard_map(
        shards, mesh=mesh, in_specs=placed, out_specs=P("queue", "head"), check_vma=False
    )
```

```python
import functools
import math

import jax
import jax.numpy as jnp
from jax import lax
from jax.experimental import pallas as pl
from jax.experimental.pallas import tpu as pltpu
from jax.sharding import PartitionSpec as P

HD = 128
XS, YS, CORES, ZH = 4, 4, 2, 2
MESH = pl.DeviceIdType.MESH
ROWS = 256
KEYS_BY_X = 3
HOPS = 8
STEPS = (
    "w0 r0 w1 r1", "r2 a0 a1 z00", "z10 r3 w2 r4", "a2 a3 z20 z30", "Y0 Y1 z01 z11", "a4 a5 z40 z50", "w3 Y2 Y3 z21", "x30 a6 a7 z31", "z02 z12 z60 z70", "Y4 z41 z51 a8", "a9 z80 z90 Y5", "x31 w4 Y6 z22", "z32 Y7 z03 z13", "z61 z71 x32 Y8", "Y9 z42 z52 z81", "z91 w5 x33 x10", "z23 z33 x20 x11", "z04 z14 z62 z72", "x12 z43 z53 x21", "x13 z82 z92 x34", "x14 w6 z24 z34", "x22 z05 z15 z63", "z73 z44 z54 x35", "x15 z83 z93 x23", "w7 z25 z35 z06", "z16 z64 z74 x24", "z45 z55 x16 z84", "z94 x36 z26 z36", "z07 z17 z65 z75", "z46 z56 x25 z85", "z95 z27 z37 x37", "f0 f1 x17 z66", "z76 F0 z47 z57", "F1 z86 z96 f2", "f3 x26 z67 z77", "F2 f4 f5 F3", "z87 z97 f6 f7", "F4 F5 f8 f9", "x27 F6 F7 o0", "o1 o2 F8 o3", "g010 g011 g012 F9", "g013 g230 g231 g233", "g232",
)


def kernel(
    zl_count,
    res_hbm, q_hbm, k_hbm, v_hbm, w_hbm, gate_ref, level_ref,
    out_hbm,
    q_ref, k_ref, v_ref, res_ref, out_ref, pk_ref, pv_ref, relay_ref, w_ref, a_ref, hop_ref, acc_ref,
    load_sem, store_sem,
    kv_send, kv_recv, relay_send, relay_recv, wz_up, wz_down, wz_recv, wx_send, wx_recv, ws_send, ws_recv,
    hop_send, hop_recv, ay_send, ay_own, ay_far,
):
    tokens, width = q_ref.shape
    heads = width // HD
    parts = tokens // ROWS
    pieces = heads * parts
    depth = w_hbm.shape[0]
    queue_count = zl_count * XS * CORES

    queue = lax.axis_index("queue")
    head = lax.axis_index("head")
    core = lax.rem(queue, CORES)
    x = lax.rem(queue // CORES, XS)
    zl = queue // (CORES * XS)
    y = head // ZH
    zh = lax.rem(head, ZH)

    sibling = (queue + 1 - 2 * core, head)
    far = head + 1 - 2 * zh

    def x_peer(k):
        return (queue + CORES * (lax.rem(x + k, XS) - x), head)

    def y_peer(k):
        return (queue, head + ZH * (lax.rem(y + k, YS) - y))

    def ring_peer(way):
        z = lax.rem(zh * zl_count + zl + way + ZH * zl_count, ZH * zl_count)
        there = z // zl_count
        return (queue + CORES * XS * (lax.rem(z, zl_count) - zl), head + there - zh), y * ZH + 1 - there

    up, down = (queue + CORES * XS, head), (queue - CORES * XS, head)
    after, before = (queue + 1, head), (queue - 1, head)
    has_up, has_down = zl < zl_count - 1, zl > 0
    has_after, has_before = queue < queue_count - 1, queue > 0
    crosses = (core == 1) & (x == XS - 1) & has_up
    by_x = (core == 1) & (x == 0) & has_up
    by_z = (core == 1) & (x == XS - 1) & has_down
    crossed = (core == 0) & (x == 0) & has_down
    over = CORES * XS - 1
    forward, back = (queue + over, head), (queue - over, head)

    def remote(src, dst, send, recv, device):
        return pltpu.make_async_remote_copy(
            src_ref=src, dst_ref=dst, send_sem=send, recv_sem=recv, device_id=device, device_id_type=MESH
        )

    def landed(ref, sem):
        pltpu.make_async_copy(ref, ref, sem).wait()

    loads = [
        pltpu.make_async_copy(src, dst, load_sem.at[i])
        for i, (src, dst) in enumerate(((q_hbm, q_ref), (k_hbm, k_ref), (v_hbm, v_ref), (res_hbm, res_ref)))
    ]
    for load in loads:
        load.start()
    block = pl.multiple_of(queue * depth, 16)
    own_w = pltpu.make_async_copy(w_hbm, w_ref.at[pl.ds(block, depth)], load_sem.at[4])
    own_w.start()

    barrier = pltpu.get_barrier_semaphore()
    greet = [sibling, ring_peer(1)[0], ring_peer(-1)[0]] + [x_peer(k) for k in (1, 3)] + [y_peer(k) for k in (1, 3)]
    for device in greet:
        pl.semaphore_signal(barrier, inc=1, device_id=device, device_id_type=MESH)
    edges = (
        (has_after, after), (has_before, before),
        (by_x | crossed, forward), (by_z | crossed, back),
    )
    for there, device in edges:
        @pl.when(there)
        def _():
            pl.semaphore_signal(barrier, inc=1, device_id=device, device_id_type=MESH)
    pl.semaphore_wait(barrier, len(greet) + sum(there.astype(jnp.int32) for there, _ in edges))

    def w_rows(zl_from, x_from, core_from):
        index = (zl_from * XS + x_from) * CORES + core_from
        return w_ref.at[pl.ds(pl.multiple_of(index * depth, 16), depth)]

    def w_up(zl_from, src):
        @pl.when(has_up)
        def _():
            remote(src, w_rows(zl_from, x, core), wz_up.at[zl_from], wz_recv.at[zl_from], up).start()

    def w_down(zl_from, src):
        @pl.when(has_down)
        def _():
            remote(src, w_rows(zl_from, x, core), wz_down.at[zl_from], wz_recv.at[zl_from], down).start()

    w_up(zl, w_hbm)
    w_down(zl, w_hbm)

    @pl.when(has_after & jnp.logical_not(crosses))
    def _():
        for h in range(heads):
            columns = pl.ds(h * HD, HD)
            remote(k_hbm.at[:, columns], pk_ref.at[h], kv_send, kv_recv.at[0, h], after).start()
            remote(v_hbm.at[:, columns], pv_ref.at[h], kv_send, kv_recv.at[1, h], after).start()

    @pl.when(crosses)
    def _():
        for h in range(heads):
            columns = pl.ds(h * HD, HD)
            first = x_peer(1) if h < KEYS_BY_X else up
            remote(k_hbm.at[:, columns], relay_ref.at[0, h], kv_send, relay_recv.at[0, h], first).start()
            remote(v_hbm.at[:, columns], relay_ref.at[1, h], kv_send, relay_recv.at[1, h], up).start()

    def pass_on(h):
        def relay(which, device):
            landed(relay_ref.at[which, h], relay_recv.at[which, h])
            dst = (pk_ref, pv_ref)[which].at[h]
            remote(relay_ref.at[which, h], dst, relay_send, kv_recv.at[which, h], device).start()

        if h < KEYS_BY_X:
            @pl.when(by_x)
            def _():
                relay(0, forward)

        @pl.when(by_z)
        def _():
            if h >= KEYS_BY_X:
                relay(0, back)
            relay(1, back)

    def w_across(zl_from, src):
        dst = w_rows(zl_from, x, core)
        for k in (1, 3):
            remote(src, dst, wx_send, wx_recv.at[k - 1, zl_from], x_peer(k)).start()
        remote(src, dst, ws_send, ws_recv, sibling).start()

    def w_both(t, work):
        @pl.when(zl >= t)
        def _():
            work(zl - t, w_up)

        if t > 0:
            @pl.when(zl + t < zl_count)
            def _():
                work(zl + t, w_down)

    def w_hop(t):
        def work(zl_from, onward):
            rows = w_rows(zl_from, x, core)
            landed(rows, wz_recv.at[zl_from])
            onward(zl_from, rows)
            w_across(zl_from, rows)

        if t == 0:
            w_across(zl, w_hbm)
        else:
            w_both(t, work)

    def w_pass(k, t):
        def work(zl_from, _):
            rows = w_rows(zl_from, lax.rem(x + XS - k, XS), core)
            landed(rows, wx_recv.at[k - 1, zl_from])
            if k == 3:
                remote(rows, rows, wx_send, wx_recv.at[1, zl_from], x_peer(3)).start()
            remote(rows, rows, ws_send, ws_recv, sibling).start()

        w_both(t, work)

    @pl.when(jnp.logical_not(has_before))
    def _():
        pk_ref[...] = jnp.zeros_like(pk_ref)
        pv_ref[...] = jnp.zeros_like(pv_ref)

    levels = lax.broadcasted_iota(jnp.int32, gate_ref.shape, 0)
    gate_row = jnp.sum(jnp.where(levels == level_ref[0], gate_ref[...], 0.0), axis=0, keepdims=True)
    blocked = jnp.where(has_before, 0.0, -1e30).astype(jnp.float32)

    for load in loads:
        load.wait()
    own_w.wait()

    def piece(source, p):
        h, part = p // parts, p % parts
        return a_ref.at[source, h, pl.ds(part * ROWS, ROWS)]

    def z_hop(p, hop):
        device, last = ring_peer(1 - 2 * (p % 2))
        src = piece(head, p)
        if hop > 0:
            src = hop_ref.at[p, hop - 1]
            landed(src, hop_recv.at[p, hop - 1])
        dst = hop_ref.at[p, hop] if hop < HOPS - 1 else piece(last, p)
        remote(src, dst, hop_send, hop_recv.at[p, hop], device).start()

    def y_send(source, p, arrived):
        for k in (1, 3):
            remote(piece(source, p), piece(source, p), ay_send, arrived.at[k - 1, p], y_peer(k)).start()

    scale = math.log2(math.e) / math.sqrt(HD)
    contract_last = (((1,), (1,)), ((), ()))

    def attend(p):
        h, part = p // parts, p % parts
        columns = pl.ds(h * HD, HD)
        rows = pl.ds(part * ROWS, ROWS)
        if part == 0:
            @pl.when(has_before)
            def _():
                landed(pk_ref.at[h], kv_recv.at[0, h])
                landed(pv_ref.at[h], kv_recv.at[1, h])

        queries = q_ref[rows, columns]
        own = lax.dot_general(queries, k_ref[:, columns], contract_last, preferred_element_type=jnp.float32) * scale
        prior = lax.dot_general(queries, pk_ref[h], contract_last, preferred_element_type=jnp.float32) * scale + blocked
        row_max = jnp.maximum(jnp.max(own, axis=1, keepdims=True), jnp.max(prior, axis=1, keepdims=True))
        own = jnp.exp2(own - row_max)
        prior = jnp.exp2(prior - row_max)
        totals = jnp.sum(own, axis=1, keepdims=True) + jnp.sum(prior, axis=1, keepdims=True)
        summed = jnp.dot(own.astype(jnp.bfloat16), v_ref[:, columns], preferred_element_type=jnp.float32)
        summed += jnp.dot(prior.astype(jnp.bfloat16), pv_ref[h], preferred_element_type=jnp.float32)
        a_ref[head, h, rows] = (summed / totals).astype(jnp.bfloat16)
        y_send(head, p, ay_own)

    def project(source, first_head, last_head, part, first=False):
        rows = pl.ds(part * ROWS, ROWS)
        deep = (last_head - first_head) * HD
        left = jnp.concatenate([a_ref[source, h, rows] for h in range(first_head, last_head)], axis=1)
        start = pl.multiple_of(source * width + first_head * HD, HD)
        term = jnp.dot(left, w_ref[pl.ds(start, deep)], preferred_element_type=jnp.float32)
        if first:
            acc_ref[rows] = term
        else:
            acc_ref[rows] += term

    def source_of(k, side):
        return ZH * lax.rem(y + YS - k, YS) + side

    seen = set()

    def y_landed(k, side, p):
        if k > 0 and (k, side is zh, p) not in seen:
            seen.add((k, side is zh, p))
            landed(piece(source_of(k, side), p), (ay_own if side is zh else ay_far).at[k - 1, p])

    def y_pass(side, p):
        k = 1 if p % 2 == 0 else 3
        y_landed(k, side, p)
        ref = piece(source_of(k, side), p)
        arrived = ay_own if side is zh else ay_far
        remote(ref, ref, ay_send, arrived.at[1, p], y_peer(k)).start()

    def project_source(k, side, first_head, last_head, part, first=False):
        for h in range(first_head, last_head):
            y_landed(k, side, h * parts + part)
        project(source_of(k, side), first_head, last_head, part, first)

    other = 1 - zh
    weights_here = False
    for step in " ".join(STEPS).split():
        kind, numbers = step[0], [int(c) for c in step[1:]]
        if kind == "a":
            attend(*numbers)
        elif kind == "r":
            pass_on(*numbers)
        elif kind == "z":
            z_hop(*numbers)
        elif kind == "f":
            landed(piece(far, numbers[0]), hop_recv.at[numbers[0], HOPS - 1])
            y_send(far, numbers[0], ay_far)
        elif kind == "Y":
            y_pass(zh, *numbers)
        elif kind == "F":
            y_pass(other, *numbers)
        elif kind == "w":
            w_hop(*numbers)
        elif kind == "x":
            w_pass(*numbers)
        else:
            if not weights_here:
                landed(w_ref.at[pl.ds(0, queue_count * depth // 2)], ws_recv)
                weights_here = True
            for part in range(parts):
                if kind == "o":
                    project_source(numbers[0], zh, 0, heads, part, first=numbers[0] == 0)
                else:
                    project_source(numbers[2], other, numbers[0], numbers[1] + 1, part)
    stores = []
    for part in range(parts):
        for k in (0, 1, 3, 2):
            project_source(k, other, heads - 1, heads, part)
        rows = pl.ds(part * ROWS, ROWS)
        out_ref[rows] = (res_ref[rows].astype(jnp.float32) + gate_row * acc_ref[rows]).astype(jnp.bfloat16)
        store = pltpu.make_async_copy(out_ref.at[rows], out_hbm.at[rows], store_sem.at[part])
        store.start()
        stores.append(store)

    @pl.when(by_x)
    def _():
        landed(relay_ref.at[0, pl.ds(0, KEYS_BY_X)], relay_send)

    @pl.when(by_z)
    def _():
        landed(relay_ref.at[1], relay_send)
        landed(relay_ref.at[0, pl.ds(KEYS_BY_X, heads - KEYS_BY_X)], relay_send)

    @pl.when(has_after)
    def _():
        landed(w_ref.at[pl.ds(0, 2 * tokens)], kv_send)

    for t in range(zl_count):
        @pl.when(has_up & (zl >= t))
        def _():
            landed(w_rows(t, x, core), wz_up.at[t])

        @pl.when(has_down & (zl <= t))
        def _():
            landed(w_rows(t, x, core), wz_down.at[t])

    landed(w_ref.at[pl.ds(0, 3 * zl_count * depth)], wx_send)
    landed(w_ref.at[pl.ds(0, XS * zl_count * depth)], ws_send)
    landed(a_ref, hop_send)
    landed(a_ref.at[pl.ds(0, 6)], ay_send)
    for store in stores:
        store.wait()


def shards(residual, queries, keys, values, out_weight, gate_table, levels):
    tokens, width = queries.shape
    heads = width // HD
    pieces = heads * (tokens // ROWS)
    sources = lax.axis_size("head")
    queue_count = lax.axis_size("queue")
    zl_count = queue_count // (XS * CORES)
    whole = out_weight.shape[0] * queue_count
    bf16 = jnp.bfloat16
    dma = pltpu.SemaphoreType.DMA
    anywhere = pl.BlockSpec(memory_space=pl.ANY)
    return pl.pallas_call(
        functools.partial(kernel, zl_count),
        out_shape=jax.ShapeDtypeStruct(residual.shape, bf16),
        in_specs=[anywhere] * 5 + [pl.BlockSpec(memory_space=pltpu.VMEM), pl.BlockSpec(memory_space=pltpu.SMEM)],
        out_specs=anywhere,
        scratch_shapes=[
            pltpu.VMEM((tokens, width), bf16),
            pltpu.VMEM((tokens, width), bf16),
            pltpu.VMEM((tokens, width), bf16),
            pltpu.VMEM((tokens, width), bf16),
            pltpu.VMEM((tokens, width), bf16),
            pltpu.VMEM((heads, tokens, HD), bf16),
            pltpu.VMEM((heads, tokens, HD), bf16),
            pltpu.VMEM((2, heads, tokens, HD), bf16),
            pltpu.VMEM((whole, width), bf16),
            pltpu.VMEM((sources, heads, tokens, HD), bf16),
            pltpu.VMEM((pieces, HOPS - 1, ROWS, HD), bf16),
            pltpu.VMEM((tokens, width), jnp.float32),
            dma((5,)),
            dma((tokens // ROWS,)),
            dma,
            dma((2, heads)),
            dma,
            dma((2, heads)),
            dma((zl_count,)),
            dma((zl_count,)),
            dma((zl_count,)),
            dma,
            dma((3, zl_count)),
            dma,
            dma,
            dma,
            dma((pieces, HOPS)),
            dma,
            dma((3, pieces)),
            dma((3, pieces)),
        ],
        compiler_params=pltpu.CompilerParams(
            collective_id=0, has_side_effects=True, vmem_limit_bytes=56 * 2**20
        ),
    )(residual, queries, keys, values, out_weight, gate_table, levels)


def solution(mesh):
    placed = (
        P("queue", "head"),
        P("queue", "head"),
        P("queue", "head"),
        P("queue", "head"),
        P("queue", "head"),
        P(None, "head"),
        P("queue"),
    )
    return jax.shard_map(
        shards, mesh=mesh, in_specs=placed, out_specs=P("queue", "head"), check_vma=False
    )
```

```python
import functools
import math

import jax
import jax.numpy as jnp
from jax import lax
from jax.experimental import pallas as pl
from jax.experimental.pallas import tpu as pltpu
from jax.sharding import PartitionSpec as P

HD = 128
XS, YS, CORES, ZH = 4, 4, 2, 2
MESH = pl.DeviceIdType.MESH
ROWS = 256
KEYS_BY_X = 3
HOPS = 8
STEPS = (
    "w0 r0 w1 r1", "r2 a0 a1 z00", "z10 r3 w2 r4", "a2 a3 z20 z30", "Y0 Y1 z01 z11", "a4 a5 z40 z50", "w3 Y2 Y3 z21", "x30 a6 a7 z31", "z02 z12 z60 z70", "Y4 z41 z51 a8", "a9 Y5 x31 w4", "Y6 z22 z32 Y7", "z03 z13 z80 z90", "z61 z71 x32 Y8", "Y9 z42 z52 w5", "z23 z33 x33 x10", "z04 z14 x20 x11", "z81 z91 z62 z72", "x12 z43 z53 x21", "x13 w6 x34 x14", "z24 z34 z05 z15", "x22 z82 z92 z63", "z73 x35 x15 z44", "z54 x23 w7 z25", "z35 z06 z16 z83", "z93 z64 z74 x36", "x16 z45 z55 z26", "z36 x24 z07 z17", "z84 z94 z65 z75", "x25 z46 z56 z27", "z37 x37 f0 f1", "x17 z85 z95 F0", "z66 z76 F1 z47", "z57 f2 f3 x26", "z86 z96 F2 z67", "z77 F3 f4 f5", "z87 z97 F4 f6", "f7 f8 f9 F5", "x27 F6 o0 F7", "o1 o2 F8 o3", "g010 g011 F9 g012", "g013 g230 g231 g233", "g232",
)


def kernel(
    zl_count,
    res_hbm, q_hbm, k_hbm, v_hbm, w_hbm, gate_ref, level_ref,
    out_ref,
    q_ref, k_ref, v_ref, res_ref, pk_ref, pv_ref, relay_ref, w_ref, a_ref, hop_ref, acc_ref,
    load_sem,
    kv_send, kv_recv, relay_send, relay_recv, wz_up, wz_down, wz_recv, wx_send, wx_recv, ws_send, ws_recv,
    hop_send, hop_recv, ay_send, ay_own, ay_far,
):
    tokens, width = q_ref.shape
    heads = width // HD
    parts = tokens // ROWS
    pieces = heads * parts
    depth = w_hbm.shape[0]
    queue_count = zl_count * XS * CORES

    queue = lax.axis_index("queue")
    head = lax.axis_index("head")
    core = lax.rem(queue, CORES)
    x = lax.rem(queue // CORES, XS)
    zl = queue // (CORES * XS)
    y = head // ZH
    zh = lax.rem(head, ZH)

    sibling = (queue + 1 - 2 * core, head)
    far = head + 1 - 2 * zh

    def x_peer(k):
        return (queue + CORES * (lax.rem(x + k, XS) - x), head)

    def y_peer(k):
        return (queue, head + ZH * (lax.rem(y + k, YS) - y))

    def ring_peer(way):
        z = lax.rem(zh * zl_count + zl + way + ZH * zl_count, ZH * zl_count)
        there = z // zl_count
        return (queue + CORES * XS * (lax.rem(z, zl_count) - zl), head + there - zh), y * ZH + 1 - there

    up, down = (queue + CORES * XS, head), (queue - CORES * XS, head)
    after, before = (queue + 1, head), (queue - 1, head)
    has_up, has_down = zl < zl_count - 1, zl > 0
    has_after, has_before = queue < queue_count - 1, queue > 0
    crosses = (core == 1) & (x == XS - 1) & has_up
    by_x = (core == 1) & (x == 0) & has_up
    by_z = (core == 1) & (x == XS - 1) & has_down
    crossed = (core == 0) & (x == 0) & has_down
    over = CORES * XS - 1
    forward, back = (queue + over, head), (queue - over, head)

    def remote(src, dst, send, recv, device):
        return pltpu.make_async_remote_copy(
            src_ref=src, dst_ref=dst, send_sem=send, recv_sem=recv, device_id=device, device_id_type=MESH
        )

    def landed(ref, sem):
        pltpu.make_async_copy(ref, ref, sem).wait()

    loads = [
        pltpu.make_async_copy(src, dst, load_sem.at[i])
        for i, (src, dst) in enumerate(((q_hbm, q_ref), (k_hbm, k_ref), (v_hbm, v_ref), (res_hbm, res_ref)))
    ]
    for load in loads:
        load.start()
    block = pl.multiple_of(queue * depth, 16)
    own_w = pltpu.make_async_copy(w_hbm, w_ref.at[pl.ds(block, depth)], load_sem.at[4])
    own_w.start()

    barrier = pltpu.get_barrier_semaphore()
    greet = [sibling, ring_peer(1)[0], ring_peer(-1)[0]] + [x_peer(k) for k in (1, 3)] + [y_peer(k) for k in (1, 3)]
    for device in greet:
        pl.semaphore_signal(barrier, inc=1, device_id=device, device_id_type=MESH)
    edges = (
        (has_after, after), (has_before, before),
        (by_x | crossed, forward), (by_z | crossed, back),
    )
    for there, device in edges:
        @pl.when(there)
        def _():
            pl.semaphore_signal(barrier, inc=1, device_id=device, device_id_type=MESH)
    pl.semaphore_wait(barrier, len(greet) + sum(there.astype(jnp.int32) for there, _ in edges))

    def w_rows(zl_from, x_from, core_from):
        index = (zl_from * XS + x_from) * CORES + core_from
        return w_ref.at[pl.ds(pl.multiple_of(index * depth, 16), depth)]

    def w_up(zl_from, src):
        @pl.when(has_up)
        def _():
            remote(src, w_rows(zl_from, x, core), wz_up.at[zl_from], wz_recv.at[zl_from], up).start()

    def w_down(zl_from, src):
        @pl.when(has_down)
        def _():
            remote(src, w_rows(zl_from, x, core), wz_down.at[zl_from], wz_recv.at[zl_from], down).start()

    w_up(zl, w_hbm)
    w_down(zl, w_hbm)

    @pl.when(has_after & jnp.logical_not(crosses))
    def _():
        for h in range(heads):
            columns = pl.ds(h * HD, HD)
            remote(k_hbm.at[:, columns], pk_ref.at[h], kv_send, kv_recv.at[0, h], after).start()
            remote(v_hbm.at[:, columns], pv_ref.at[h], kv_send, kv_recv.at[1, h], after).start()

    @pl.when(crosses)
    def _():
        for h in range(heads):
            columns = pl.ds(h * HD, HD)
            first = x_peer(1) if h < KEYS_BY_X else up
            remote(k_hbm.at[:, columns], relay_ref.at[0, h], kv_send, relay_recv.at[0, h], first).start()
            remote(v_hbm.at[:, columns], relay_ref.at[1, h], kv_send, relay_recv.at[1, h], up).start()

    def pass_on(h):
        def relay(which, device):
            landed(relay_ref.at[which, h], relay_recv.at[which, h])
            dst = (pk_ref, pv_ref)[which].at[h]
            remote(relay_ref.at[which, h], dst, relay_send, kv_recv.at[which, h], device).start()

        if h < KEYS_BY_X:
            @pl.when(by_x)
            def _():
                relay(0, forward)

        @pl.when(by_z)
        def _():
            if h >= KEYS_BY_X:
                relay(0, back)
            relay(1, back)

    def w_across(zl_from, src):
        dst = w_rows(zl_from, x, core)
        for k in (1, 3):
            remote(src, dst, wx_send, wx_recv.at[k - 1, zl_from], x_peer(k)).start()
        remote(src, dst, ws_send, ws_recv, sibling).start()

    def w_both(t, work):
        @pl.when(zl >= t)
        def _():
            work(zl - t, w_up)

        if t > 0:
            @pl.when(zl + t < zl_count)
            def _():
                work(zl + t, w_down)

    def w_hop(t):
        def work(zl_from, onward):
            rows = w_rows(zl_from, x, core)
            landed(rows, wz_recv.at[zl_from])
            onward(zl_from, rows)
            w_across(zl_from, rows)

        if t == 0:
            w_across(zl, w_hbm)
        else:
            w_both(t, work)

    def w_pass(k, t):
        def work(zl_from, _):
            rows = w_rows(zl_from, lax.rem(x + XS - k, XS), core)
            landed(rows, wx_recv.at[k - 1, zl_from])
            if k == 3:
                remote(rows, rows, wx_send, wx_recv.at[1, zl_from], x_peer(3)).start()
            remote(rows, rows, ws_send, ws_recv, sibling).start()

        w_both(t, work)

    @pl.when(jnp.logical_not(has_before))
    def _():
        pk_ref[...] = jnp.zeros_like(pk_ref)
        pv_ref[...] = jnp.zeros_like(pv_ref)

    levels = lax.broadcasted_iota(jnp.int32, gate_ref.shape, 0)
    gate_row = jnp.sum(jnp.where(levels == level_ref[0], gate_ref[...], 0.0), axis=0, keepdims=True)
    blocked = jnp.where(has_before, 0.0, -1e30).astype(jnp.float32)

    for load in loads:
        load.wait()
    own_w.wait()

    def piece(source, p):
        h, part = p // parts, p % parts
        return a_ref.at[source, h, pl.ds(part * ROWS, ROWS)]

    def z_hop(p, hop):
        device, last = ring_peer(1 - 2 * (p % 2))
        src = piece(head, p)
        if hop > 0:
            src = hop_ref.at[p, hop - 1]
            landed(src, hop_recv.at[p, hop - 1])
        dst = hop_ref.at[p, hop] if hop < HOPS - 1 else piece(last, p)
        remote(src, dst, hop_send, hop_recv.at[p, hop], device).start()

    def y_send(source, p, arrived):
        for k in (1, 3):
            remote(piece(source, p), piece(source, p), ay_send, arrived.at[k - 1, p], y_peer(k)).start()

    scale = math.log2(math.e) / math.sqrt(HD)
    contract_last = (((1,), (1,)), ((), ()))

    def attend(p):
        h, part = p // parts, p % parts
        columns = pl.ds(h * HD, HD)
        rows = pl.ds(part * ROWS, ROWS)
        if part == 0:
            @pl.when(has_before)
            def _():
                landed(pk_ref.at[h], kv_recv.at[0, h])
                landed(pv_ref.at[h], kv_recv.at[1, h])

        queries = q_ref[rows, columns]
        own = lax.dot_general(queries, k_ref[:, columns], contract_last, preferred_element_type=jnp.float32) * scale
        prior = lax.dot_general(queries, pk_ref[h], contract_last, preferred_element_type=jnp.float32) * scale + blocked
        row_max = jnp.maximum(jnp.max(own, axis=1, keepdims=True), jnp.max(prior, axis=1, keepdims=True))
        own = jnp.exp2(own - row_max)
        prior = jnp.exp2(prior - row_max)
        totals = jnp.sum(own, axis=1, keepdims=True) + jnp.sum(prior, axis=1, keepdims=True)
        summed = jnp.dot(own.astype(jnp.bfloat16), v_ref[:, columns], preferred_element_type=jnp.float32)
        summed += jnp.dot(prior.astype(jnp.bfloat16), pv_ref[h], preferred_element_type=jnp.float32)
        a_ref[head, h, rows] = (summed / totals).astype(jnp.bfloat16)
        y_send(head, p, ay_own)

    def project(source, first_head, last_head, part, first=False):
        rows = pl.ds(part * ROWS, ROWS)
        deep = (last_head - first_head) * HD
        left = jnp.concatenate([a_ref[source, h, rows] for h in range(first_head, last_head)], axis=1)
        start = pl.multiple_of(source * width + first_head * HD, HD)
        term = jnp.dot(left, w_ref[pl.ds(start, deep)], preferred_element_type=jnp.float32)
        if first:
            acc_ref[rows] = term
        else:
            acc_ref[rows] += term

    def source_of(k, side):
        return ZH * lax.rem(y + YS - k, YS) + side

    seen = set()

    def y_landed(k, side, p):
        if k > 0 and (k, side is zh, p) not in seen:
            seen.add((k, side is zh, p))
            landed(piece(source_of(k, side), p), (ay_own if side is zh else ay_far).at[k - 1, p])

    def y_pass(side, p):
        k = 1 if p % 2 == 0 else 3
        y_landed(k, side, p)
        ref = piece(source_of(k, side), p)
        arrived = ay_own if side is zh else ay_far
        remote(ref, ref, ay_send, arrived.at[1, p], y_peer(k)).start()

    def project_source(k, side, first_head, last_head, part, first=False):
        for h in range(first_head, last_head):
            y_landed(k, side, h * parts + part)
        project(source_of(k, side), first_head, last_head, part, first)

    other = 1 - zh
    weights_here = False
    for step in " ".join(STEPS).split():
        kind, numbers = step[0], [int(c) for c in step[1:]]
        if kind == "a":
            attend(*numbers)
        elif kind == "r":
            pass_on(*numbers)
        elif kind == "z":
            z_hop(*numbers)
        elif kind == "f":
            landed(piece(far, numbers[0]), hop_recv.at[numbers[0], HOPS - 1])
            y_send(far, numbers[0], ay_far)
        elif kind == "Y":
            y_pass(zh, *numbers)
        elif kind == "F":
            y_pass(other, *numbers)
        elif kind == "w":
            w_hop(*numbers)
        elif kind == "x":
            w_pass(*numbers)
        else:
            if not weights_here:
                landed(w_ref.at[pl.ds(0, queue_count * depth // 2)], ws_recv)
                weights_here = True
            for part in range(parts):
                if kind == "o":
                    project_source(numbers[0], zh, 0, heads, part, first=numbers[0] == 0)
                else:
                    project_source(numbers[2], other, numbers[0], numbers[1] + 1, part)
    for part in range(parts):
        for k in (0, 1, 3, 2):
            project_source(k, other, heads - 1, heads, part)
        rows = pl.ds(part * ROWS, ROWS)
        out_ref[rows] = (res_ref[rows].astype(jnp.float32) + gate_row * acc_ref[rows]).astype(jnp.bfloat16)

    @pl.when(by_x)
    def _():
        landed(relay_ref.at[0, pl.ds(0, KEYS_BY_X)], relay_send)

    @pl.when(by_z)
    def _():
        landed(relay_ref.at[1], relay_send)
        landed(relay_ref.at[0, pl.ds(KEYS_BY_X, heads - KEYS_BY_X)], relay_send)

    @pl.when(has_after)
    def _():
        landed(w_ref.at[pl.ds(0, 2 * tokens)], kv_send)

    for t in range(zl_count):
        @pl.when(has_up & (zl >= t))
        def _():
            landed(w_rows(t, x, core), wz_up.at[t])

        @pl.when(has_down & (zl <= t))
        def _():
            landed(w_rows(t, x, core), wz_down.at[t])

    landed(w_ref.at[pl.ds(0, 3 * zl_count * depth)], wx_send)
    landed(w_ref.at[pl.ds(0, XS * zl_count * depth)], ws_send)
    landed(a_ref, hop_send)
    landed(a_ref.at[pl.ds(0, 6)], ay_send)


def shards(residual, queries, keys, values, out_weight, gate_table, levels):
    tokens, width = queries.shape
    heads = width // HD
    pieces = heads * (tokens // ROWS)
    sources = lax.axis_size("head")
    queue_count = lax.axis_size("queue")
    zl_count = queue_count // (XS * CORES)
    whole = out_weight.shape[0] * queue_count
    bf16 = jnp.bfloat16
    dma = pltpu.SemaphoreType.DMA
    anywhere = pl.BlockSpec(memory_space=pl.ANY)
    return pl.pallas_call(
        functools.partial(kernel, zl_count),
        out_shape=jax.ShapeDtypeStruct(residual.shape, bf16),
        in_specs=[anywhere] * 5 + [pl.BlockSpec(memory_space=pltpu.VMEM), pl.BlockSpec(memory_space=pltpu.SMEM)],
        out_specs=pl.BlockSpec(memory_space=pltpu.VMEM),
        scratch_shapes=[
            pltpu.VMEM((tokens, width), bf16),
            pltpu.VMEM((tokens, width), bf16),
            pltpu.VMEM((tokens, width), bf16),
            pltpu.VMEM((tokens, width), bf16),
            pltpu.VMEM((heads, tokens, HD), bf16),
            pltpu.VMEM((heads, tokens, HD), bf16),
            pltpu.VMEM((2, heads, tokens, HD), bf16),
            pltpu.VMEM((whole, width), bf16),
            pltpu.VMEM((sources, heads, tokens, HD), bf16),
            pltpu.VMEM((pieces, HOPS - 1, ROWS, HD), bf16),
            pltpu.VMEM((tokens, width), jnp.float32),
            dma((5,)),
            dma,
            dma((2, heads)),
            dma,
            dma((2, heads)),
            dma((zl_count,)),
            dma((zl_count,)),
            dma((zl_count,)),
            dma,
            dma((3, zl_count)),
            dma,
            dma,
            dma,
            dma((pieces, HOPS)),
            dma,
            dma((3, pieces)),
            dma((3, pieces)),
        ],
        compiler_params=pltpu.CompilerParams(
            collective_id=0, has_side_effects=True, vmem_limit_bytes=56 * 2**20
        ),
    )(residual, queries, keys, values, out_weight, gate_table, levels)


def solution(mesh):
    placed = (
        P("queue", "head"),
        P("queue", "head"),
        P("queue", "head"),
        P("queue", "head"),
        P("queue", "head"),
        P(None, "head"),
        P("queue"),
    )
    return jax.shard_map(
        shards, mesh=mesh, in_specs=placed, out_specs=P("queue", "head"), check_vma=False
    )
```

```python
import functools
import math

import jax
import jax.numpy as jnp
from jax import lax
from jax.experimental import pallas as pl
from jax.experimental.pallas import tpu as pltpu
from jax.sharding import PartitionSpec as P

HD = 128
XS, YS, CORES, ZH = 4, 4, 2, 2
MESH = pl.DeviceIdType.MESH
ROWS = 256
KEYS_BY_X = 3
HOPS = 8
STEPS = (
    "w0 r0 w1 r1", "r2 a0 a1 z00", "z10 r3 w2 r4", "a2 a3 z20 z30", "Y0 Y1 z01 z11", "a4 a5 z40 z50", "w3 Y2 Y3 z21", "x30 a6 a7 z31", "z02 z12 z60 z70", "Y4 z41 z51 a8", "a9 Y5 x31 w4", "Y6 z22 z32 Y7", "z03 z13 z80 z90", "z61 z71 x32 Y8", "Y9 z42 z52 w5", "z23 z33 x33 x10", "z04 z14 x20 x11", "z81 z91 z62 z72", "x12 z43 z53 x21", "x13 w6 x34 x14", "z24 z34 z05 z15", "x22 z82 z92 z63", "z73 x35 x15 z44", "z54 x23 w7 z25", "z35 z06 z16 z83", "z93 z64 z74 x36", "x16 z45 z55 z26", "z36 x24 z07 z17", "z84 z94 z65 z75", "x25 z46 z56 z27", "z37 x37 f0 f1", "x17 z85 z95 F0", "z66 z76 F1 z47", "z57 f2 f3 x26", "z86 z96 F2 z67", "z77 F3 f4 f5", "z87 z97 F4 f6", "f7 f8 f9 F5", "x27 F6 o0 F7", "o1 o2 F8 o3", "g010 g011 F9 g012", "g013 g230 g231 g233", "g232",
)


def kernel(
    zl_count,
    res_hbm, q_hbm, k_hbm, v_hbm, w_hbm, gate_ref, level_ref,
    out_ref,
    q_ref, k_ref, v_ref, res_ref, pk_ref, pv_ref, relay_ref, w_ref, a_ref, hop_ref, acc_ref,
    load_sem,
    kv_send, kv_recv, relay_send, relay_recv, wz_up, wz_down, wz_recv, wx_send, wx_recv, ws_send, ws_recv,
    hop_send, hop_recv, ay_send, ay_own, ay_far,
):
    tokens, width = q_ref.shape
    heads = width // HD
    parts = tokens // ROWS
    pieces = heads * parts
    depth = w_hbm.shape[0]
    queue_count = zl_count * XS * CORES

    queue = lax.axis_index("queue")
    head = lax.axis_index("head")
    core = lax.rem(queue, CORES)
    x = lax.rem(queue // CORES, XS)
    zl = queue // (CORES * XS)
    y = head // ZH
    zh = lax.rem(head, ZH)

    sibling = (queue + 1 - 2 * core, head)
    far = head + 1 - 2 * zh

    def x_peer(k):
        return (queue + CORES * (lax.rem(x + k, XS) - x), head)

    def y_peer(k):
        return (queue, head + ZH * (lax.rem(y + k, YS) - y))

    def ring_peer(way):
        z = lax.rem(zh * zl_count + zl + way + ZH * zl_count, ZH * zl_count)
        there = z // zl_count
        return (queue + CORES * XS * (lax.rem(z, zl_count) - zl), head + there - zh), y * ZH + 1 - there

    up, down = (queue + CORES * XS, head), (queue - CORES * XS, head)
    after, before = (queue + 1, head), (queue - 1, head)
    has_up, has_down = zl < zl_count - 1, zl > 0
    has_after, has_before = queue < queue_count - 1, queue > 0
    crosses = (core == 1) & (x == XS - 1) & has_up
    by_x = (core == 1) & (x == 0) & has_up
    by_z = (core == 1) & (x == XS - 1) & has_down
    crossed = (core == 0) & (x == 0) & has_down
    over = CORES * XS - 1
    forward, back = (queue + over, head), (queue - over, head)

    def remote(src, dst, send, recv, device):
        return pltpu.make_async_remote_copy(
            src_ref=src, dst_ref=dst, send_sem=send, recv_sem=recv, device_id=device, device_id_type=MESH
        )

    def landed(ref, sem):
        pltpu.make_async_copy(ref, ref, sem).wait()

    loads = [
        pltpu.make_async_copy(src, dst, load_sem.at[i])
        for i, (src, dst) in enumerate(((q_hbm, q_ref), (k_hbm, k_ref), (v_hbm, v_ref), (res_hbm, res_ref)))
    ]
    for load in loads:
        load.start()
    block = pl.multiple_of(queue * depth, 16)
    own_w = pltpu.make_async_copy(w_hbm, w_ref.at[pl.ds(block, depth)], load_sem.at[4])
    own_w.start()

    barrier = pltpu.get_barrier_semaphore()
    greet = [sibling, ring_peer(1)[0], ring_peer(-1)[0]] + [x_peer(k) for k in (1, 3)] + [y_peer(k) for k in (1, 2, 3)]
    for device in greet:
        pl.semaphore_signal(barrier, inc=1, device_id=device, device_id_type=MESH)
    edges = (
        (has_after, after), (has_before, before),
        (by_x | crossed, forward), (by_z | crossed, back),
    )
    for there, device in edges:
        @pl.when(there)
        def _():
            pl.semaphore_signal(barrier, inc=1, device_id=device, device_id_type=MESH)
    pl.semaphore_wait(barrier, len(greet) + sum(there.astype(jnp.int32) for there, _ in edges))

    def w_rows(zl_from, x_from, core_from):
        index = (zl_from * XS + x_from) * CORES + core_from
        return w_ref.at[pl.ds(pl.multiple_of(index * depth, 16), depth)]

    def w_up(zl_from, src):
        @pl.when(has_up)
        def _():
            remote(src, w_rows(zl_from, x, core), wz_up.at[zl_from], wz_recv.at[zl_from], up).start()

    def w_down(zl_from, src):
        @pl.when(has_down)
        def _():
            remote(src, w_rows(zl_from, x, core), wz_down.at[zl_from], wz_recv.at[zl_from], down).start()

    w_up(zl, w_hbm)
    w_down(zl, w_hbm)

    @pl.when(has_after & jnp.logical_not(crosses))
    def _():
        for h in range(heads):
            columns = pl.ds(h * HD, HD)
            remote(k_hbm.at[:, columns], pk_ref.at[h], kv_send, kv_recv.at[0, h], after).start()
            remote(v_hbm.at[:, columns], pv_ref.at[h], kv_send, kv_recv.at[1, h], after).start()

    @pl.when(crosses)
    def _():
        for h in range(heads):
            columns = pl.ds(h * HD, HD)
            first = x_peer(1) if h < KEYS_BY_X else up
            remote(k_hbm.at[:, columns], relay_ref.at[0, h], kv_send, relay_recv.at[0, h], first).start()
            remote(v_hbm.at[:, columns], relay_ref.at[1, h], kv_send, relay_recv.at[1, h], up).start()

    def pass_on(h):
        def relay(which, device):
            landed(relay_ref.at[which, h], relay_recv.at[which, h])
            dst = (pk_ref, pv_ref)[which].at[h]
            remote(relay_ref.at[which, h], dst, relay_send, kv_recv.at[which, h], device).start()

        if h < KEYS_BY_X:
            @pl.when(by_x)
            def _():
                relay(0, forward)

        @pl.when(by_z)
        def _():
            if h >= KEYS_BY_X:
                relay(0, back)
            relay(1, back)

    def w_across(zl_from, src):
        dst = w_rows(zl_from, x, core)
        for k in (1, 3):
            remote(src, dst, wx_send, wx_recv.at[k - 1, zl_from], x_peer(k)).start()
        remote(src, dst, ws_send, ws_recv, sibling).start()

    def w_both(t, work):
        @pl.when(zl >= t)
        def _():
            work(zl - t, w_up)

        if t > 0:
            @pl.when(zl + t < zl_count)
            def _():
                work(zl + t, w_down)

    def w_hop(t):
        def work(zl_from, onward):
            rows = w_rows(zl_from, x, core)
            landed(rows, wz_recv.at[zl_from])
            onward(zl_from, rows)
            w_across(zl_from, rows)

        if t == 0:
            w_across(zl, w_hbm)
        else:
            w_both(t, work)

    def w_pass(k, t):
        def work(zl_from, _):
            rows = w_rows(zl_from, lax.rem(x + XS - k, XS), core)
            landed(rows, wx_recv.at[k - 1, zl_from])
            if k == 3:
                remote(rows, rows, wx_send, wx_recv.at[1, zl_from], x_peer(3)).start()
            remote(rows, rows, ws_send, ws_recv, sibling).start()

        w_both(t, work)

    @pl.when(jnp.logical_not(has_before))
    def _():
        pk_ref[...] = jnp.zeros_like(pk_ref)
        pv_ref[...] = jnp.zeros_like(pv_ref)

    levels = lax.broadcasted_iota(jnp.int32, gate_ref.shape, 0)
    gate_row = jnp.sum(jnp.where(levels == level_ref[0], gate_ref[...], 0.0), axis=0, keepdims=True)
    blocked = jnp.where(has_before, 0.0, -1e30).astype(jnp.float32)

    for load in loads:
        load.wait()
    own_w.wait()

    def piece(source, p):
        h, part = p // parts, p % parts
        return a_ref.at[source, h, pl.ds(part * ROWS, ROWS)]

    def z_hop(p, hop):
        device, last = ring_peer(1 - 2 * (p % 2))
        src = piece(head, p)
        if hop > 0:
            src = hop_ref.at[p, hop - 1]
            landed(src, hop_recv.at[p, hop - 1])
        dst = hop_ref.at[p, hop] if hop < HOPS - 1 else piece(last, p)
        remote(src, dst, hop_send, hop_recv.at[p, hop], device).start()

    def y_send(source, p, arrived):
        direct = arrived is ay_far and p >= pieces - parts
        for k in (2, 1, 3) if direct else (1, 3):
            remote(piece(source, p), piece(source, p), ay_send, arrived.at[k - 1, p], y_peer(k)).start()

    scale = math.log2(math.e) / math.sqrt(HD)
    contract_last = (((1,), (1,)), ((), ()))

    def attend(p):
        h, part = p // parts, p % parts
        columns = pl.ds(h * HD, HD)
        rows = pl.ds(part * ROWS, ROWS)
        if part == 0:
            @pl.when(has_before)
            def _():
                landed(pk_ref.at[h], kv_recv.at[0, h])
                landed(pv_ref.at[h], kv_recv.at[1, h])

        queries = q_ref[rows, columns]
        own = lax.dot_general(queries, k_ref[:, columns], contract_last, preferred_element_type=jnp.float32) * scale
        prior = lax.dot_general(queries, pk_ref[h], contract_last, preferred_element_type=jnp.float32) * scale + blocked
        row_max = jnp.maximum(jnp.max(own, axis=1, keepdims=True), jnp.max(prior, axis=1, keepdims=True))
        own = jnp.exp2(own - row_max)
        prior = jnp.exp2(prior - row_max)
        totals = jnp.sum(own, axis=1, keepdims=True) + jnp.sum(prior, axis=1, keepdims=True)
        summed = jnp.dot(own.astype(jnp.bfloat16), v_ref[:, columns], preferred_element_type=jnp.float32)
        summed += jnp.dot(prior.astype(jnp.bfloat16), pv_ref[h], preferred_element_type=jnp.float32)
        a_ref[head, h, rows] = (summed / totals).astype(jnp.bfloat16)
        y_send(head, p, ay_own)

    def project(source, first_head, last_head, part, first=False):
        rows = pl.ds(part * ROWS, ROWS)
        deep = (last_head - first_head) * HD
        left = jnp.concatenate([a_ref[source, h, rows] for h in range(first_head, last_head)], axis=1)
        start = pl.multiple_of(source * width + first_head * HD, HD)
        term = jnp.dot(left, w_ref[pl.ds(start, deep)], preferred_element_type=jnp.float32)
        if first:
            acc_ref[rows] = term
        else:
            acc_ref[rows] += term

    def source_of(k, side):
        return ZH * lax.rem(y + YS - k, YS) + side

    seen = set()

    def y_landed(k, side, p):
        if k > 0 and (k, side is zh, p) not in seen:
            seen.add((k, side is zh, p))
            landed(piece(source_of(k, side), p), (ay_own if side is zh else ay_far).at[k - 1, p])

    def y_pass(side, p):
        if side is not zh and p >= pieces - parts:
            return
        k = 1 if p % 2 == 0 else 3
        y_landed(k, side, p)
        ref = piece(source_of(k, side), p)
        arrived = ay_own if side is zh else ay_far
        remote(ref, ref, ay_send, arrived.at[1, p], y_peer(k)).start()

    def project_source(k, side, first_head, last_head, part, first=False):
        for h in range(first_head, last_head):
            y_landed(k, side, h * parts + part)
        project(source_of(k, side), first_head, last_head, part, first)

    other = 1 - zh
    weights_here = False
    for step in " ".join(STEPS).split():
        kind, numbers = step[0], [int(c) for c in step[1:]]
        if kind == "a":
            attend(*numbers)
        elif kind == "r":
            pass_on(*numbers)
        elif kind == "z":
            z_hop(*numbers)
        elif kind == "f":
            landed(piece(far, numbers[0]), hop_recv.at[numbers[0], HOPS - 1])
            y_send(far, numbers[0], ay_far)
        elif kind == "Y":
            y_pass(zh, *numbers)
        elif kind == "F":
            y_pass(other, *numbers)
        elif kind == "w":
            w_hop(*numbers)
        elif kind == "x":
            w_pass(*numbers)
        else:
            if not weights_here:
                landed(w_ref.at[pl.ds(0, queue_count * depth // 2)], ws_recv)
                weights_here = True
            for part in range(parts):
                if kind == "o":
                    project_source(numbers[0], zh, 0, heads, part, first=numbers[0] == 0)
                else:
                    project_source(numbers[2], other, numbers[0], numbers[1] + 1, part)
    for part in range(parts):
        for k in (0, 1, 3, 2):
            project_source(k, other, heads - 1, heads, part)
        rows = pl.ds(part * ROWS, ROWS)
        out_ref[rows] = (res_ref[rows].astype(jnp.float32) + gate_row * acc_ref[rows]).astype(jnp.bfloat16)

    @pl.when(by_x)
    def _():
        landed(relay_ref.at[0, pl.ds(0, KEYS_BY_X)], relay_send)

    @pl.when(by_z)
    def _():
        landed(relay_ref.at[1], relay_send)
        landed(relay_ref.at[0, pl.ds(KEYS_BY_X, heads - KEYS_BY_X)], relay_send)

    @pl.when(has_after)
    def _():
        landed(w_ref.at[pl.ds(0, 2 * tokens)], kv_send)

    for t in range(zl_count):
        @pl.when(has_up & (zl >= t))
        def _():
            landed(w_rows(t, x, core), wz_up.at[t])

        @pl.when(has_down & (zl <= t))
        def _():
            landed(w_rows(t, x, core), wz_down.at[t])

    landed(w_ref.at[pl.ds(0, 3 * zl_count * depth)], wx_send)
    landed(w_ref.at[pl.ds(0, XS * zl_count * depth)], ws_send)
    landed(a_ref, hop_send)
    landed(a_ref.at[pl.ds(0, 6)], ay_send)


def shards(residual, queries, keys, values, out_weight, gate_table, levels):
    tokens, width = queries.shape
    heads = width // HD
    pieces = heads * (tokens // ROWS)
    sources = lax.axis_size("head")
    queue_count = lax.axis_size("queue")
    zl_count = queue_count // (XS * CORES)
    whole = out_weight.shape[0] * queue_count
    bf16 = jnp.bfloat16
    dma = pltpu.SemaphoreType.DMA
    anywhere = pl.BlockSpec(memory_space=pl.ANY)
    return pl.pallas_call(
        functools.partial(kernel, zl_count),
        out_shape=jax.ShapeDtypeStruct(residual.shape, bf16),
        in_specs=[anywhere] * 5 + [pl.BlockSpec(memory_space=pltpu.VMEM), pl.BlockSpec(memory_space=pltpu.SMEM)],
        out_specs=pl.BlockSpec(memory_space=pltpu.VMEM),
        scratch_shapes=[
            pltpu.VMEM((tokens, width), bf16),
            pltpu.VMEM((tokens, width), bf16),
            pltpu.VMEM((tokens, width), bf16),
            pltpu.VMEM((tokens, width), bf16),
            pltpu.VMEM((heads, tokens, HD), bf16),
            pltpu.VMEM((heads, tokens, HD), bf16),
            pltpu.VMEM((2, heads, tokens, HD), bf16),
            pltpu.VMEM((whole, width), bf16),
            pltpu.VMEM((sources, heads, tokens, HD), bf16),
            pltpu.VMEM((pieces, HOPS - 1, ROWS, HD), bf16),
            pltpu.VMEM((tokens, width), jnp.float32),
            dma((5,)),
            dma,
            dma((2, heads)),
            dma,
            dma((2, heads)),
            dma((zl_count,)),
            dma((zl_count,)),
            dma((zl_count,)),
            dma,
            dma((3, zl_count)),
            dma,
            dma,
            dma,
            dma((pieces, HOPS)),
            dma,
            dma((3, pieces)),
            dma((3, pieces)),
        ],
        compiler_params=pltpu.CompilerParams(
            collective_id=0, has_side_effects=True, vmem_limit_bytes=56 * 2**20
        ),
    )(residual, queries, keys, values, out_weight, gate_table, levels)


def solution(mesh):
    placed = (
        P("queue", "head"),
        P("queue", "head"),
        P("queue", "head"),
        P("queue", "head"),
        P("queue", "head"),
        P(None, "head"),
        P("queue"),
    )
    return jax.shard_map(
        shards, mesh=mesh, in_specs=placed, out_specs=P("queue", "head"), check_vma=False
    )
```
